512 devices in a mesh: grp: 4 (over x), row: 128 (over y, z, core).
Axes of the slice: x: 4, y: 8, z: 8, core: 2. Of those that a mesh axis runs over, the one named last changes fastest.
Arguments:
- sketch: float32 [393216, 512], P('row', 'grp'), may hold values from -600 to 600, as said below
Outputs:
- basis: float32 [393216, 512], P(('row', 'grp'))
- upper: float32 [512, 512], replicated
The draws below stay inside these ranges and needn't reach their ends.
Inputs may be any that keep to these rules, and one draw needn't show every extreme that they name: `sketch`: real values, the columns linearly independent.
All inputs are finite; a program needn't handle non-finite values.
Results may differ from the reference program's by a relative error of at most 0.000075.
Values sent between devices are 32-bit elements; how exact they have to be, the bound alone decides.
No kernel may reach another device: no remote copies, remote signals or barrier semaphores. Data moves between devices by JAX's collectives and lax.ppermute only.
A program may use at most 128 MiB of HBM per device.

```python
import jax
import jax.numpy as jnp
from jax import lax

K = 512
ROWS = 393216


def draw_sketch(key, part):
    keys = jax.random.split(key, 3)
    row_scale = jnp.exp(jax.random.uniform(keys[0], (ROWS, 1), jnp.float32, 0.0, 2.302585))
    base = jax.random.truncated_normal(keys[1], -4.0, 4.0, (ROWS, K), jnp.float32)
    col_scale = jnp.exp(jax.random.uniform(keys[2], (1, K), jnp.float32, 0.0, 1.6))
    values = base * row_scale * col_scale
    return values.astype(jnp.float32)


def setup_inputs(seed: int = 0) -> dict:
    seeds = jax.random.split(jax.random.key(seed), 2)
    sketch = draw_sketch(jax.random.fold_in(seeds[1], 71), 0)
    return dict(sketch=sketch)


def reference(sketch):
    gram = lax.dot_general(sketch.astype(jnp.float32), sketch.astype(jnp.float32), (((0,), (0,)), ((), ())), precision=lax.Precision.HIGHEST, preferred_element_type=jnp.float32) / jnp.float32(ROWS)
    lower = jnp.linalg.cholesky(gram)
    upper = lower.T
    identity = jnp.eye(K, dtype=jnp.float32)
    inverse = lax.linalg.triangular_solve(upper, identity, left_side=True, lower=False)
    basis = jnp.dot(sketch.astype(jnp.float32), inverse.astype(jnp.float32), precision=lax.Precision.HIGHEST, preferred_element_type=jnp.float32)
    return (basis, upper)
```

```python
import functools

import jax
import jax.numpy as jnp
from jax import lax
from jax.experimental import pallas as pl
from jax.experimental.pallas import tpu as pltpu
from jax.sharding import Mesh
from jax.sharding import PartitionSpec as P

B = 128
N = 512
STEPS = N // B
PAIRS = [(k, j) for k in range(STEPS) for j in range(k, STEPS)]
HALF = len(PAIRS) // 2
F32 = jnp.float32
SMEM = pl.BlockSpec(memory_space=pltpu.SMEM)
VMEM = pl.BlockSpec(memory_space=pltpu.VMEM)


def dot(left, right, left_dim=1, right_dim=0):
    return lax.dot_general(
        left,
        right,
        (((left_dim,), (right_dim,)), ((), ())),
        precision=lax.Precision.HIGHEST,
        preferred_element_type=F32,
    )


def factor_block(rows):
    count = len(rows)
    rows = list(rows)
    lane = lax.broadcasted_iota(jnp.int32, (8, B), 1)
    sub = lax.broadcasted_iota(jnp.int32, (8, B), 0)

    def spread(v):
        return jnp.broadcast_to(v, (8, B))

    upper, inverse = [], []
    for p in range(count):
        c0 = 8 * p
        cols = {q: [spread(rows[q][:, c0 + s : c0 + s + 1]) for s in range(8)] for q in range(p, count)}
        inside = (lane >= c0) & (lane < c0 + 8)
        rows[p] = jnp.where(inside, jnp.where(lane - c0 == sub, 1.0, 0.0), rows[p])
        for q in range(p + 1, count):
            rows[q] = jnp.where(inside, 0.0, rows[q])
        pivots = jnp.zeros((8, B), F32)
        for s in range(8):
            pivot = spread(cols[p][s][s : s + 1])
            pivots = jnp.where(sub == s, pivot, pivots)
            scale = 1.0 / pivot
            ahead = [spread(cols[p][t][s : s + 1]) if t > s else None for t in range(8)]
            row = spread(rows[p][s : s + 1])
            for q in range(p, count):
                factor = cols[q][s] * scale
                if q == p:
                    factor = jnp.where(sub > s, factor, 0.0)
                for t in range(s + 1, 8):
                    cols[q][t] = cols[q][t] - factor * ahead[t]
                rows[q] = rows[q] - factor * row
        root = lax.rsqrt(pivots)
        root = root * (1.5 - 0.5 * pivots * root * root)
        u = rows[p]
        for t in range(8):
            u = jnp.where(lane == c0 + t, cols[p][t], u)
        upper.append(jnp.where(lane >= c0 + sub, u, 0.0) * root)
        inverse.append(jnp.where(lane <= c0 + sub, rows[p], 0.0) * root)
    return jnp.concatenate(upper, 0), jnp.concatenate(inverse, 0)


def gram_kernel(scale, core, x, mine, theirs, parts):
    for k in range(STEPS):
        for j in range(k, STEPS):
            parts[PAIRS.index((k, j))] = dot(x[k], x[j], 0, 0) * scale
    mine[...] = parts[pl.ds(core[0] * HALF, HALF)].reshape(HALF * B, B)
    theirs[...] = parts[pl.ds((1 - core[0]) * HALF, HALF)].reshape(HALF * B, B)


def gram(core, x, scale):
    return pl.pallas_call(
        functools.partial(gram_kernel, scale),
        in_specs=[SMEM, VMEM],
        out_shape=[jax.ShapeDtypeStruct((HALF * B, B), F32)] * 2,
        scratch_shapes=[pltpu.VMEM((len(PAIRS), B, B), F32)],
        compiler_params=pltpu.CompilerParams(vmem_limit_bytes=32 << 20),
        name="gram",
    )(core, x)


def factor_kernel(core, mine, theirs, x, basis_ref, u_ref, m):
    for k in range(STEPS):
        for j in range(STEPS):
            here = (slice(k * B, k * B + B), slice(j * B, j * B + B))
            if j >= k:
                owner, at = divmod(PAIRS.index((k, j)), HALF)
                rows = slice(at * B, at * B + B)
                m[here] = jnp.where(core[0] == owner, mine[rows, :], theirs[rows, :])
            else:
                m[here] = jnp.zeros((B, B), F32)
    block = lax.broadcasted_iota(jnp.int32, (B, N), 1) // B

    @pl.loop(0, STEPS)
    def _(k):
        o = pl.multiple_of(k * B, B)
        here = pl.ds(o, B)
        uk, ik = factor_block([m[pl.ds(o + 8 * q, 8), here] for q in range(B // 8)])
        panel = dot(ik, m[here, :])
        m[here, :] = panel
        m[here, here] = ik
        u_ref[here, :] = jnp.where(block > k, panel, 0.0)
        u_ref[here, here] = uk
        for i in range(1, STEPS):
            rows = slice(i * B, i * B + B)

            @pl.when(i > k)
            def _():
                m[rows, :] = jnp.where(block == k, 0.0, m[rows, :]) - dot(u_ref[here, rows], m[here, :], 0, 0)

    for j in range(STEPS):
        total = dot(x[0], m[j * B : j * B + B, :B], 1, 1)
        for g in range(1, j + 1):
            total = total + dot(x[g], m[j * B : j * B + B, g * B : g * B + B], 1, 1)
        basis_ref[:, j * B : j * B + B] = total


def factor(core, mine, theirs, x):
    return pl.pallas_call(
        factor_kernel,
        in_specs=[SMEM, VMEM, VMEM, VMEM],
        out_shape=[jax.ShapeDtypeStruct((x.shape[1], N), F32), jax.ShapeDtypeStruct((N, N), F32)],
        scratch_shapes=[pltpu.VMEM((N, N), F32)],
        compiler_params=pltpu.CompilerParams(vmem_limit_bytes=32 << 20),
        name="factor",
    )(core, mine, theirs, x)


def other_core(v):
    return lax.ppermute(v, "core", [(0, 1), (1, 0)])


def from_x(v, d):
    count = lax.axis_size("x")
    return lax.ppermute(v, "x", [(i, (i + d) % count) for i in range(count)])


def all_sum(mine, theirs):
    mine = mine + other_core(theirs)
    rows = mine.shape[0]
    peers = lax.axis_size(("y", "z"))
    pieces = mine.reshape(peers, rows // peers, B)
    pieces = lax.all_to_all(pieces, ("y", "z"), split_axis=0, concat_axis=0, tiled=True)
    piece = jnp.sum(pieces, axis=0)
    total = (piece + from_x(piece, 2)) + (from_x(piece, 1) + from_x(piece, 3))
    pieces = jnp.broadcast_to(total[None], (peers,) + total.shape)
    pieces = lax.all_to_all(pieces, ("y", "z"), split_axis=0, concat_axis=0, tiled=True)
    mine = pieces.reshape(rows, B)
    return mine, other_core(mine)


def local(sketch):
    groups = lax.axis_size("x")
    x = lax.all_to_all(sketch.reshape(groups, -1, B), "x", split_axis=0, concat_axis=0, tiled=True)
    total_rows = x.shape[1] * lax.axis_size(("x", "y", "z", "core"))
    core = lax.axis_index("core").reshape(1)
    mine, theirs = gram(core, x, 1.0 / total_rows)
    mine, theirs = all_sum(mine, theirs)
    return factor(core, mine, theirs, x)


def solution(mesh):
    grp, row = mesh.devices.shape
    core = 2
    side = 8
    grid = Mesh(mesh.devices.reshape(grp, row // (side * core), side, core), ("x", "y", "z", "core"))
    row_axes = ("y", "z", "core")
    return jax.shard_map(
        local,
        mesh=grid,
        in_specs=(P(row_axes, "x"),),
        out_specs=(P(row_axes + ("x",), None), P()),
        check_vma=False,
    )
```

```python
import functools

import jax
import jax.numpy as jnp
from jax import lax
from jax.experimental import pallas as pl
from jax.experimental.pallas import tpu as pltpu
from jax.sharding import Mesh
from jax.sharding import PartitionSpec as P

B = 128
N = 512
STEPS = N // B
PAIRS = [(k, j) for k in range(STEPS) for j in range(k, STEPS)]
HALF = len(PAIRS) // 2
F32 = jnp.float32
BF16 = jnp.bfloat16
NEAR = 3
SMEM = pl.BlockSpec(memory_space=pltpu.SMEM)
VMEM = pl.BlockSpec(memory_space=pltpu.VMEM)


def dot(left, right, left_dim=1, right_dim=0):
    return lax.dot_general(
        left,
        right,
        (((left_dim,), (right_dim,)), ((), ())),
        precision=lax.Precision.HIGHEST,
        preferred_element_type=F32,
    )


def split(v):
    high = v.astype(BF16).astype(F32)
    rest = v - high
    middle = rest.astype(BF16).astype(F32)
    return high, middle, rest - middle


def wide_dot(left, right, left_dim, right_dim):
    a, b, c = split(left)
    d, e, f = split(right)
    left = jnp.concatenate([a, a, b, b, a, c], left_dim).astype(BF16)
    right = jnp.concatenate([d, e, d, e, f, d], right_dim).astype(BF16)
    return lax.dot_general(left, right, (((left_dim,), (right_dim,)), ((), ())), preferred_element_type=F32)


def factor_block(rows, after):
    count = len(rows)
    rows = list(rows)
    lane = lax.broadcasted_iota(jnp.int32, (8, B), 1)
    sub = lax.broadcasted_iota(jnp.int32, (8, B), 0)

    def spread(v):
        return jnp.broadcast_to(v, (8, B))

    def columns(q, first):
        return [spread(rows[q][:, first + s : first + s + 1]) for s in range(8)]

    upper, inverse = [], []
    coming = columns(0, 0)
    for p in range(count):
        c0 = 8 * p
        inside = (lane >= c0) & (lane < c0 + 8)
        cols = coming
        own = jnp.where(inside, jnp.where(lane - c0 == sub, 1.0, 0.0), rows[p])
        last = p + 1 == count
        below = None if last else columns(p + 1, c0)
        coming = None if last else columns(p + 1, c0 + 8)
        pivots = jnp.zeros((8, B), F32)
        scales, ahead, pivot_rows = [], [], []
        for s in range(8):
            pivot = spread(cols[s][s : s + 1])
            pivots = jnp.where(sub == s, pivot, pivots)
            scales.append(1.0 / pivot)
            ahead.append([spread(cols[t][s : s + 1]) if t > s else None for t in range(8)])
            pivot_rows.append(spread(own[s : s + 1]))
            factor = jnp.where(sub > s, cols[s], 0.0) * scales[s]
            for t in range(s + 1, 8):
                cols[t] = cols[t] - factor * ahead[s][t]
            own = own - factor * pivot_rows[s]
        for q in range(p + 1, min(count, p + 1 + NEAR)):
            here = below if q == p + 1 else columns(q, c0)
            target = jnp.where(inside, 0.0, rows[q])
            for s in range(8):
                factor = here[s] * scales[s]
                for t in range(s + 1, 8):
                    here[t] = here[t] - factor * ahead[s][t]
                if q == p + 1:
                    coming = [coming[t] - factor * spread(here[s][t : t + 1]) for t in range(8)]
                target = target - factor * pivot_rows[s]
            rows[q] = target
        root = lax.rsqrt(pivots)
        root = root * (1.5 - 0.5 * pivots * root * root)
        scaled = own * root
        far = p + 1 + NEAR
        if far < count:
            update = wide_dot(scaled, scaled, 0, 0)
            for q in range(far, count):
                rows[q] = jnp.where(inside, 0.0, rows[q]) - update[8 * q : 8 * q + 8]
        u = own
        for t in range(8):
            u = jnp.where(lane == c0 + t, cols[t], u)
        upper.append(jnp.where(lane >= c0 + sub, u, 0.0) * root)
        inverse.append(jnp.where(lane <= c0 + sub, scaled, 0.0))
        after(p)
    return jnp.concatenate(upper, 0), jnp.concatenate(inverse, 0)


def gram_kernel(scale, core, x, mine, theirs, parts):
    wide = [jnp.concatenate([x[2 * h], x[2 * h + 1]], 1) for h in range(2)]
    for h, i in ((0, 0), (0, 1), (1, 1)):
        product = dot(wide[h], wide[i], 0, 0) * scale
        for k in (2 * h, 2 * h + 1):
            for j in (2 * i, 2 * i + 1):
                if j >= k:
                    parts[PAIRS.index((k, j))] = product[k % 2 * B : k % 2 * B + B, j % 2 * B : j % 2 * B + B]
    mine[...] = parts[pl.ds(core[0] * HALF, HALF)].reshape(HALF * B, B)
    theirs[...] = parts[pl.ds((1 - core[0]) * HALF, HALF)].reshape(HALF * B, B)


def gram(core, x, scale):
    return pl.pallas_call(
        functools.partial(gram_kernel, scale),
        in_specs=[SMEM, VMEM],
        out_shape=[jax.ShapeDtypeStruct((HALF * B, B), F32)] * 2,
        scratch_shapes=[pltpu.VMEM((len(PAIRS), B, B), F32)],
        compiler_params=pltpu.CompilerParams(vmem_limit_bytes=32 << 20),
        name="gram",
    )(core, x)


def factor_kernel(core, mine, theirs, x, basis_ref, u_ref, m):
    todo = []

    def after(p):
        for _ in range(-(-len(todo) // (B // 8 - p))):
            todo.pop(0)()

    def block(k):
        return slice(k * B, k * B + B)

    def panel(k, j, inverse):
        r = wide_dot(inverse, m[block(k), block(j)], 1, 0)
        m[block(k), block(j)] = r
        if j > k:
            u_ref[block(k), block(j)] = r

    def trail(k, i, j):
        d = wide_dot(u_ref[block(k), block(i)], m[block(k), block(j)], 0, 0)
        m[block(i), block(j)] = -d if j == k else m[block(i), block(j)] - d

    def basis(h, rows):
        cols = slice(2 * h * B, 2 * h * B + 2 * B)
        m[block(2 * h), block(2 * h + 1)] = jnp.zeros((B, B), F32)
        left = jnp.concatenate([x[g, rows, :] for g in range(2 * h + 2)], 1)
        basis_ref[rows, cols] = dot(left, m[cols, : cols.stop], 1, 1)

    for k, j in PAIRS:
        owner, at = divmod(PAIRS.index((k, j)), HALF)
        m[block(k), block(j)] = jnp.where(core[0] == owner, mine[block(at), :], theirs[block(at), :])
    for k in range(STEPS):
        rows = [m[k * B + 8 * q : k * B + 8 * q + 8, block(k)] for q in range(B // 8)]
        upper, inverse = factor_block(rows, after)
        u_ref[block(k), block(k)] = upper
        for j in range(k):
            u_ref[block(k), block(j)] = jnp.zeros((B, B), F32)
        if k + 1 < STEPS:
            panel(k, k + 1, inverse)
            trail(k, k + 1, k + 1)
        m[block(k), block(k)] = inverse
        todo += [functools.partial(panel, k, j, inverse) for j in range(STEPS) if j not in (k, k + 1)]
        for i in range(k + 1, STEPS):
            for j in range(STEPS):
                if (j <= k or j >= i) and (i, j) != (k + 1, k + 1):
                    todo.append(functools.partial(trail, k, i, j))
        if k == STEPS // 2:
            todo += [functools.partial(basis, 0, slice(c, c + 2 * B)) for c in range(0, x.shape[1], 2 * B)]
    todo += [functools.partial(basis, 1, slice(0, x.shape[1]))]
    while todo:
        todo.pop(0)()


def factor(core, mine, theirs, x):
    return pl.pallas_call(
        factor_kernel,
        in_specs=[SMEM, VMEM, VMEM, VMEM],
        out_shape=[jax.ShapeDtypeStruct((x.shape[1], N), F32), jax.ShapeDtypeStruct((N, N), F32)],
        scratch_shapes=[pltpu.VMEM((N, N), F32)],
        compiler_params=pltpu.CompilerParams(vmem_limit_bytes=32 << 20),
        name="factor",
    )(core, mine, theirs, x)


def other_core(v):
    return lax.ppermute(v, "core", [(0, 1), (1, 0)])


def from_x(v, d):
    count = lax.axis_size("x")
    return lax.ppermute(v, "x", [(i, (i + d) % count) for i in range(count)])


def all_sum(mine, theirs):
    mine = mine + other_core(theirs)
    rows = mine.shape[0]
    peers = lax.axis_size(("y", "z"))
    pieces = mine.reshape(peers, rows // peers // 2, 2, B)
    pieces = lax.all_to_all(pieces, ("y", "z"), split_axis=0, concat_axis=0, tiled=True)
    piece = jnp.sum(pieces, axis=0)
    total = (piece + from_x(piece, 2)) + (from_x(piece, 1) + from_x(piece, 3))
    pieces = jnp.broadcast_to(total[None], (peers,) + total.shape)
    pieces = lax.all_to_all(pieces, ("y", "z"), split_axis=0, concat_axis=0, tiled=True)
    mine = pieces.reshape(rows, B)
    return mine, other_core(mine)


def local(sketch):
    groups = lax.axis_size("x")
    x = lax.all_to_all(sketch.reshape(groups, -1, B), "x", split_axis=0, concat_axis=0, tiled=True)
    total_rows = x.shape[1] * lax.axis_size(("x", "y", "z", "core"))
    core = lax.axis_index("core").reshape(1)
    mine, theirs = gram(core, x, 1.0 / total_rows)
    mine, theirs = all_sum(mine, theirs)
    return factor(core, mine, theirs, x)


def solution(mesh):
    grp, row = mesh.devices.shape
    core = 2
    side = 8
    grid = Mesh(mesh.devices.reshape(grp, row // (side * core), side, core), ("x", "y", "z", "core"))
    row_axes = ("y", "z", "core")
    return jax.shard_map(
        local,
        mesh=grid,
        in_specs=(P(row_axes, "x"),),
        out_specs=(P(row_axes + ("x",), None), P()),
        check_vma=False,
    )
```

```python
import functools

import jax
import jax.numpy as jnp
from jax import lax
from jax.experimental import pallas as pl
from jax.experimental.pallas import tpu as pltpu
from jax.sharding import Mesh
from jax.sharding import PartitionSpec as P

B = 128
N = 512
STEPS = N // B
PAIRS = [(k, j) for k in range(STEPS) for j in range(k, STEPS)]
HALF = len(PAIRS) // 2
F32 = jnp.float32
BF16 = jnp.bfloat16
NEAR = 3
SMEM = pl.BlockSpec(memory_space=pltpu.SMEM)
VMEM = pl.BlockSpec(memory_space=pltpu.VMEM)


def dot(left, right, left_dim=1, right_dim=0):
    return lax.dot_general(
        left,
        right,
        (((left_dim,), (right_dim,)), ((), ())),
        precision=lax.Precision.HIGHEST,
        preferred_element_type=F32,
    )


def split(v):
    high = v.astype(BF16).astype(F32)
    rest = v - high
    middle = rest.astype(BF16).astype(F32)
    return high, middle, rest - middle


def wide_dot(left, right, left_dim, right_dim):
    a, b, c = split(left)
    d, e, f = split(right)
    left = jnp.concatenate([a, a, b, b, a, c], left_dim).astype(BF16)
    right = jnp.concatenate([d, e, d, e, f, d], right_dim).astype(BF16)
    return lax.dot_general(left, right, (((left_dim,), (right_dim,)), ((), ())), preferred_element_type=F32)


def factor_block(rows, after):
    count = len(rows)
    rows = list(rows)
    lane = lax.broadcasted_iota(jnp.int32, (8, B), 1)
    sub = lax.broadcasted_iota(jnp.int32, (8, B), 0)

    def spread(v):
        return jnp.broadcast_to(v, (8, B))

    def columns(q, first):
        return [spread(rows[q][:, first + s : first + s + 1]) for s in range(8)]

    upper, inverse = [], []
    coming = columns(0, 0)
    for p in range(count):
        c0 = 8 * p
        inside = (lane >= c0) & (lane < c0 + 8)
        cols = coming
        own = jnp.where(inside, jnp.where(lane - c0 == sub, 1.0, 0.0), rows[p])
        last = p + 1 == count
        below = None if last else columns(p + 1, c0)
        coming = None if last else columns(p + 1, c0 + 8)
        pivots = jnp.zeros((8, B), F32)
        scales, ahead, pivot_rows = [], [], []
        for s in range(8):
            pivot = spread(cols[s][s : s + 1])
            pivots = jnp.where(sub == s, pivot, pivots)
            scales.append(1.0 / pivot)
            ahead.append([spread(cols[t][s : s + 1]) if t > s else None for t in range(8)])
            pivot_rows.append(spread(own[s : s + 1]))
            factor = jnp.where(sub > s, cols[s], 0.0) * scales[s]
            for t in range(s + 1, 8):
                cols[t] = cols[t] - factor * ahead[s][t]
            own = own - factor * pivot_rows[s]
        for q in range(p + 1, min(count, p + 1 + NEAR)):
            here = below if q == p + 1 else columns(q, c0)
            target = jnp.where(inside, 0.0, rows[q])
            for s in range(8):
                factor = here[s] * scales[s]
                for t in range(s + 1, 8):
                    here[t] = here[t] - factor * ahead[s][t]
                if q == p + 1:
                    coming = [coming[t] - factor * spread(here[s][t : t + 1]) for t in range(8)]
                target = target - factor * pivot_rows[s]
            rows[q] = target
        root = lax.rsqrt(pivots)
        root = root * (1.5 - 0.5 * pivots * root * root)
        scaled = own * root
        far = p + 1 + NEAR
        if far < count:
            update = wide_dot(scaled, scaled, 0, 0)
            for q in range(far, count):
                rows[q] = jnp.where(inside, 0.0, rows[q]) - update[8 * q : 8 * q + 8]
        u = own
        for t in range(8):
            u = jnp.where(lane == c0 + t, cols[t], u)
        upper.append(jnp.where(lane >= c0 + sub, u, 0.0) * root)
        inverse.append(jnp.where(lane <= c0 + sub, scaled, 0.0))
        after(p)
    return jnp.concatenate(upper, 0), jnp.concatenate(inverse, 0)


def gram_kernel(scale, core, x, mine, theirs, parts):
    wide = [jnp.concatenate([x[2 * h], x[2 * h + 1]], 1) for h in range(2)]
    for h, i in ((0, 0), (0, 1), (1, 1)):
        product = dot(wide[h], wide[i], 0, 0) * scale
        for k in (2 * h, 2 * h + 1):
            for j in (2 * i, 2 * i + 1):
                if j >= k:
                    parts[PAIRS.index((k, j))] = product[k % 2 * B : k % 2 * B + B, j % 2 * B : j % 2 * B + B]
    mine[...] = parts[pl.ds(core[0] * HALF, HALF)].reshape(HALF * B, B)
    theirs[...] = parts[pl.ds((1 - core[0]) * HALF, HALF)].reshape(HALF * B, B)


def gram(core, x, scale):
    return pl.pallas_call(
        functools.partial(gram_kernel, scale),
        in_specs=[SMEM, VMEM],
        out_shape=[jax.ShapeDtypeStruct((HALF * B, B), F32)] * 2,
        scratch_shapes=[pltpu.VMEM((len(PAIRS), B, B), F32)],
        compiler_params=pltpu.CompilerParams(vmem_limit_bytes=32 << 20),
        name="gram",
    )(core, x)


def factor_kernel(core, mine, theirs, x, basis_ref, u_ref, m):
    todo = []

    def after(p):
        for _ in range(-(-len(todo) // (B // 8 - p))):
            todo.pop(0)()

    def block(k):
        return slice(k * B, k * B + B)

    def panel(k, j, inverse):
        r = wide_dot(inverse, m[block(k), block(j)], 1, 0)
        m[block(k), block(j)] = r
        if j > k:
            u_ref[block(k), block(j)] = r

    def trail(k, i, j):
        d = wide_dot(u_ref[block(k), block(i)], m[block(k), block(j)], 0, 0)
        m[block(i), block(j)] = -d if j == k else m[block(i), block(j)] - d

    def basis(h, rows):
        cols = slice(2 * h * B, 2 * h * B + 2 * B)
        m[block(2 * h), block(2 * h + 1)] = jnp.zeros((B, B), F32)
        left = jnp.concatenate([x[g, rows, :] for g in range(2 * h + 2)], 1)
        basis_ref[rows, cols] = dot(left, m[cols, : cols.stop], 1, 1)

    for k, j in PAIRS:
        owner, at = divmod(PAIRS.index((k, j)), HALF)
        m[block(k), block(j)] = jnp.where(core[0] == owner, mine[block(at), :], theirs[block(at), :])
    for k in range(STEPS):
        rows = [m[k * B + 8 * q : k * B + 8 * q + 8, block(k)] for q in range(B // 8)]
        upper, inverse = factor_block(rows, after)
        u_ref[block(k), block(k)] = upper
        for j in range(k):
            u_ref[block(k), block(j)] = jnp.zeros((B, B), F32)
        if k + 1 < STEPS:
            panel(k, k + 1, inverse)
            trail(k, k + 1, k + 1)
        m[block(k), block(k)] = inverse
        todo += [functools.partial(panel, k, j, inverse) for j in range(STEPS) if j not in (k, k + 1)]
        for i in range(k + 1, STEPS):
            for j in range(STEPS):
                if (j <= k or j >= i) and (i, j) != (k + 1, k + 1):
                    todo.append(functools.partial(trail, k, i, j))
        if k == STEPS // 2:
            todo += [functools.partial(basis, 0, slice(c, c + 2 * B)) for c in range(0, x.shape[1], 2 * B)]
    todo += [functools.partial(basis, 1, slice(0, x.shape[1]))]
    while todo:
        todo.pop(0)()


def factor(core, mine, theirs, x):
    return pl.pallas_call(
        factor_kernel,
        in_specs=[SMEM, VMEM, VMEM, VMEM],
        out_shape=[jax.ShapeDtypeStruct((x.shape[1], N), F32), jax.ShapeDtypeStruct((N, N), F32)],
        scratch_shapes=[pltpu.VMEM((N, N), F32)],
        compiler_params=pltpu.CompilerParams(vmem_limit_bytes=32 << 20),
        name="factor",
    )(core, mine, theirs, x)


def other_core(v):
    return lax.ppermute(v, "core", [(0, 1), (1, 0)])


def all_sum(mine, theirs):
    chips = ("x", "y", "z")
    mine = mine + other_core(theirs)
    rows = mine.shape[0]
    peers = lax.axis_size(chips)
    share = -(-rows // peers)
    pieces = jnp.concatenate([mine, jnp.zeros((share * peers - rows, B), F32)], 0).reshape(peers, share, 1, B)
    pieces = lax.all_to_all(pieces, chips, split_axis=0, concat_axis=0, tiled=True)
    piece = jnp.sum(pieces, axis=0)
    pieces = jnp.broadcast_to(piece[None], (peers,) + piece.shape)
    pieces = lax.all_to_all(pieces, chips, split_axis=0, concat_axis=0, tiled=True)
    mine = pieces.reshape(share * peers, B)
    return mine[:rows], other_core(mine[:rows])


def local(sketch):
    groups = lax.axis_size("x")
    x = lax.all_to_all(sketch.reshape(groups, -1, B), "x", split_axis=0, concat_axis=0, tiled=True)
    total_rows = x.shape[1] * lax.axis_size(("x", "y", "z", "core"))
    core = lax.axis_index("core").reshape(1)
    mine, theirs = gram(core, x, 1.0 / total_rows)
    mine, theirs = all_sum(mine, theirs)
    return factor(core, mine, theirs, x)


def solution(mesh):
    grp, row = mesh.devices.shape
    core = 2
    side = 8
    grid = Mesh(mesh.devices.reshape(grp, row // (side * core), side, core), ("x", "y", "z", "core"))
    row_axes = ("y", "z", "core")
    return jax.shard_map(
        local,
        mesh=grid,
        in_specs=(P(row_axes, "x"),),
        out_specs=(P(row_axes + ("x",), None), P()),
        check_vma=False,
    )
```

```python
import functools

import jax
import jax.numpy as jnp
from jax import lax
from jax.experimental import pallas as pl
from jax.experimental.pallas import tpu as pltpu
from jax.sharding import Mesh
from jax.sharding import PartitionSpec as P

B = 128
N = 512
STEPS = N // B
PAIRS = [(k, j) for k in range(STEPS) for j in range(k, STEPS)]
BOTH = 2
HALF = (len(PAIRS) - BOTH) // 2
OWN = BOTH + HALF
F32 = jnp.float32
BF16 = jnp.bfloat16
NEAR = 3
SMEM = pl.BlockSpec(memory_space=pltpu.SMEM)
VMEM = pl.BlockSpec(memory_space=pltpu.VMEM)


def split(v):
    high = v.astype(BF16).astype(F32)
    rest = v - high
    middle = rest.astype(BF16).astype(F32)
    return high, middle, rest - middle


def lay_left(parts, dim):
    a, b, c = parts
    return jnp.concatenate([a, a, b, b, a, c], dim).astype(BF16)


def lay_right(parts, dim):
    a, b, c = parts
    return jnp.concatenate([a, b, a, b, c, a], dim).astype(BF16)


def parts_dot(left, right, left_dim=1, right_dim=0):
    return lax.dot_general(left, right, (((left_dim,), (right_dim,)), ((), ())), preferred_element_type=F32)


def wide_dot(left, right, left_dim, right_dim):
    return parts_dot(lay_left(split(left), left_dim), lay_right(split(right), right_dim), left_dim, right_dim)


def factor_block(rows, after):
    count = len(rows)
    rows = list(rows)
    lane = lax.broadcasted_iota(jnp.int32, (8, B), 1)
    sub = lax.broadcasted_iota(jnp.int32, (8, B), 0)

    def spread(v):
        return jnp.broadcast_to(v, (8, B))

    def columns(q, first):
        return [spread(rows[q][:, first + s : first + s + 1]) for s in range(8)]

    upper, inverse = [], []
    coming = columns(0, 0)
    for p in range(count):
        c0 = 8 * p
        inside = (lane >= c0) & (lane < c0 + 8)
        cols = coming
        own = jnp.where(inside, jnp.where(lane - c0 == sub, 1.0, 0.0), rows[p])
        last = p + 1 == count
        below = None if last else columns(p + 1, c0)
        coming = None if last else columns(p + 1, c0 + 8)
        pivots = jnp.zeros((8, B), F32)
        scales, ahead, pivot_rows = [], [], []
        for s in range(8):
            pivot = spread(cols[s][s : s + 1])
            pivots = jnp.where(sub == s, pivot, pivots)
            scales.append(1.0 / pivot)
            ahead.append([spread(cols[t][s : s + 1]) if t > s else None for t in range(8)])
            pivot_rows.append(spread(own[s : s + 1]))
            factor = jnp.where(sub > s, cols[s], 0.0) * scales[s]
            for t in range(s + 1, 8):
                cols[t] = cols[t] - factor * ahead[s][t]
            own = own - factor * pivot_rows[s]
        for q in range(p + 1, min(count, p + 1 + NEAR)):
            here = below if q == p + 1 else columns(q, c0)
            target = jnp.where(inside, 0.0, rows[q])
            for s in range(8):
                factor = here[s] * scales[s]
                for t in range(s + 1, 8):
                    here[t] = here[t] - factor * ahead[s][t]
                if q == p + 1:
                    coming = [coming[t] - factor * spread(here[s][t : t + 1]) for t in range(8)]
                target = target - factor * pivot_rows[s]
            rows[q] = target
        root = lax.rsqrt(pivots)
        root = root * (1.5 - 0.5 * pivots * root * root)
        scaled = own * root
        far = p + 1 + NEAR
        if far < count:
            update = wide_dot(scaled, scaled, 0, 0)
            for q in range(far, count):
                rows[q] = jnp.where(inside, 0.0, rows[q]) - update[8 * q : 8 * q + 8]
        u = own
        for t in range(8):
            u = jnp.where(lane == c0 + t, cols[t], u)
        upper.append(jnp.where(lane >= c0 + sub, u, 0.0) * root)
        inverse.append(jnp.where(lane <= c0 + sub, scaled, 0.0))
        after(p)
    return jnp.concatenate(upper, 0), jnp.concatenate(inverse, 0)


def gram_kernel(scale, core, x, mine, theirs, x_parts, parts):
    for h in range(STEPS // 2):
        for i, part in enumerate(split(jnp.concatenate([x[2 * h], x[2 * h + 1]], 1))):
            x_parts[i, :, 2 * h * B : 2 * h * B + 2 * B] = part.astype(BF16)
    wide = [[x_parts[i, :, 2 * h * B : 2 * h * B + 2 * B] for i in range(3)] for h in range(STEPS // 2)]
    turned = [lay_left([part.T for part in parts], 1) for parts in wide]
    for h, i in ((0, 0), (0, 1), (1, 1)):
        product = parts_dot(turned[h], lay_right(wide[i], 0)) * scale
        for k in (2 * h, 2 * h + 1):
            for j in (2 * i, 2 * i + 1):
                if j >= k:
                    parts[PAIRS.index((k, j))] = product[k % 2 * B : k % 2 * B + B, j % 2 * B : j % 2 * B + B]
    for owner, out in ((core[0], mine), (1 - core[0], theirs)):
        out[: BOTH * B, :] = parts[:BOTH].reshape(BOTH * B, B)
        out[BOTH * B :, :] = parts[pl.ds(BOTH + owner * HALF, HALF)].reshape(HALF * B, B)


def gram(core, x, scale):
    return pl.pallas_call(
        functools.partial(gram_kernel, scale),
        in_specs=[SMEM, VMEM],
        out_shape=[jax.ShapeDtypeStruct((OWN * B, B), F32)] * 2 + [jax.ShapeDtypeStruct((3, x.shape[1], N), BF16)],
        scratch_shapes=[pltpu.VMEM((len(PAIRS), B, B), F32)],
        compiler_params=pltpu.CompilerParams(vmem_limit_bytes=32 << 20),
        name="gram",
    )(core, x)


def first_kernel(mine, upper_ref, inverse_ref, panel_ref):
    upper, inverse = factor_block([mine[8 * q : 8 * q + 8, :] for q in range(B // 8)], lambda p: None)
    upper_ref[...] = upper
    inverse_ref[...] = inverse
    panel_ref[...] = wide_dot(inverse, mine[B : 2 * B, :], 1, 0)


def first(mine):
    return pl.pallas_call(
        first_kernel,
        in_specs=[VMEM],
        out_shape=[jax.ShapeDtypeStruct((B, B), F32)] * 3,
        compiler_params=pltpu.CompilerParams(vmem_limit_bytes=16 << 20),
        cost_estimate=pl.CostEstimate(flops=4 << 20, bytes_accessed=4 << 20, transcendentals=0),
        name="first",
    )(mine)


def factor_kernel(core, mine, theirs, upper0, inverse0, panel0, x, x_parts, basis_ref, u_ref, m, rest, right):
    todo = []

    def after(p):
        for _ in range(-(-len(todo) // (B // 8 - p))):
            todo.pop(0)()

    def block(k):
        return slice(k * B, k * B + B)

    def panel(k, j, inverse):
        r = wide_dot(inverse, m[block(k), block(j)], 1, 0)
        m[block(k), block(j)] = r
        if j > k:
            u_ref[block(k), block(j)] = r

    def trail(k, i, j):
        d = wide_dot(u_ref[block(k), block(i)], m[block(k), block(j)], 0, 0)
        m[block(i), block(j)] = -d if j == k else m[block(i), block(j)] - d

    def prepare(first_row, columns):
        v = m[first_row : first_row + 2 * B, :columns]
        right[:, : 6 * columns] = lay_right(split(v), 1)

    def product(rows, columns):
        left = lay_left([x_parts[i, rows, :columns] for i in range(3)], 1)
        return parts_dot(left, right[:, : 6 * columns], 1, 1)

    def basis_first(rows):
        basis_ref[rows, : 2 * B] = product(rows, 2 * B)

    def basis_last(rows):
        both = product(rows, 3 * B)
        basis_ref[rows, block(2)] = both[:, :B]
        rest[rows, :] = both[:, B:] + x[3, rows, :]

    chunks = [slice(c, c + 2 * B) for c in range(0, x.shape[1], 2 * B)]
    for k, j in PAIRS[BOTH:]:
        owner, at = divmod(PAIRS.index((k, j)) - BOTH, HALF)
        m[block(k), block(j)] = jnp.where(core[0] == owner, mine[block(BOTH + at), :], theirs[block(at), :])
    for k in range(STEPS):
        if k == 0:
            upper, inverse = upper0[...], inverse0[...]
        else:
            rows = [m[k * B + 8 * q : k * B + 8 * q + 8, block(k)] for q in range(B // 8)]
            upper, inverse = factor_block(rows, after)
        u_ref[block(k), block(k)] = upper
        for j in range(k):
            u_ref[block(k), block(j)] = jnp.zeros((B, B), F32)
        if k == 0:
            m[block(0), block(1)] = panel0[...]
            u_ref[block(0), block(1)] = panel0[...]
        elif k + 1 < STEPS:
            panel(k, k + 1, inverse)
        if k + 1 < STEPS:
            trail(k, k + 1, k + 1)
        m[block(k), block(k)] = inverse
        if k + 1 < STEPS:
            todo += [functools.partial(panel, k, j, inverse) for j in range(STEPS) if j not in (k, k + 1)]
        for i in range(k + 1, STEPS):
            for j in range(STEPS):
                if (j <= k or j >= i) and (i, j) != (k + 1, k + 1):
                    todo.append(functools.partial(trail, k, i, j))
        if k == 1:
            m[block(0), block(1)] = jnp.zeros((B, B), F32)
            todo.append(functools.partial(prepare, 0, 2 * B))
            todo += [functools.partial(basis_first, rows) for rows in chunks]
        if k == 2:
            todo.append(functools.partial(prepare, 2 * B, 3 * B))
            todo += [functools.partial(basis_last, rows) for rows in chunks]
    basis_ref[:, block(3)] = wide_dot(rest[...], inverse, 1, 1)


def factor(core, mine, theirs, upper0, inverse0, panel0, x, x_parts):
    return pl.pallas_call(
        factor_kernel,
        in_specs=[SMEM] + [VMEM] * 7,
        out_shape=[jax.ShapeDtypeStruct((x.shape[1], N), F32), jax.ShapeDtypeStruct((N, N), F32)],
        scratch_shapes=[
            pltpu.VMEM((N, N), F32),
            pltpu.VMEM((x.shape[1], B), F32),
            pltpu.VMEM((2 * B, 6 * 3 * B), BF16),
        ],
        compiler_params=pltpu.CompilerParams(vmem_limit_bytes=32 << 20),
        name="factor",
    )(core, mine, theirs, upper0, inverse0, panel0, x, x_parts)


def other_core(v):
    return lax.ppermute(v, "core", [(0, 1), (1, 0)])


def all_sum(mine, theirs):
    chips = ("x", "y", "z")
    mine = mine + other_core(theirs)
    peers = lax.axis_size(chips)
    pieces = mine.reshape(peers, OWN * B // peers, 1, B)
    pieces = lax.all_to_all(pieces, chips, split_axis=0, concat_axis=0, tiled=True)
    piece = jnp.sum(pieces, axis=0)
    pieces = jnp.broadcast_to(piece[None], (peers,) + piece.shape)
    pieces = lax.all_to_all(pieces, chips, split_axis=0, concat_axis=0, tiled=True)
    return pieces.reshape(OWN * B, B)


def local(sketch):
    groups = lax.axis_size("x")
    x = lax.all_to_all(sketch.reshape(groups, -1, B), "x", split_axis=0, concat_axis=0, tiled=True)
    total_rows = x.shape[1] * lax.axis_size(("x", "y", "z", "core"))
    core = lax.axis_index("core").reshape(1)
    mine, theirs, x_parts = gram(core, x, 1.0 / total_rows)
    mine = all_sum(mine, theirs)
    theirs = other_core(mine[BOTH * B :])
    return factor(core, mine, theirs, *first(mine), x, x_parts)


def solution(mesh):
    grp, row = mesh.devices.shape
    core = 2
    side = 8
    grid = Mesh(mesh.devices.reshape(grp, row // (side * core), side, core), ("x", "y", "z", "core"))
    row_axes = ("y", "z", "core")
    return jax.shard_map(
        local,
        mesh=grid,
        in_specs=(P(row_axes, "x"),),
        out_specs=(P(row_axes + ("x",), None), P()),
        check_vma=False,
    )
```

```python
import functools

import jax
import jax.numpy as jnp
from jax import lax
from jax.experimental import pallas as pl
from jax.experimental.pallas import tpu as pltpu
from jax.sharding import Mesh
from jax.sharding import PartitionSpec as P

B = 128
N = 512
STEPS = N // B
PAIRS = [(k, j) for k in range(STEPS) for j in range(k, STEPS)]
BOTH = 2
HALF = (len(PAIRS) - BOTH) // 2
OWN = BOTH + HALF
F32 = jnp.float32
BF16 = jnp.bfloat16
NEAR = 3
SMEM = pl.BlockSpec(memory_space=pltpu.SMEM)
VMEM = pl.BlockSpec(memory_space=pltpu.VMEM)


def split(v):
    high = v.astype(BF16).astype(F32)
    rest = v - high
    middle = rest.astype(BF16).astype(F32)
    return high, middle, rest - middle


def lay_left(parts, dim):
    a, b, c = parts
    return jnp.concatenate([a, a, b, b, a, c], dim).astype(BF16)


def lay_right(parts, dim):
    a, b, c = parts
    return jnp.concatenate([a, b, a, b, c, a], dim).astype(BF16)


def parts_dot(left, right, left_dim=1, right_dim=0):
    return lax.dot_general(left, right, (((left_dim,), (right_dim,)), ((), ())), preferred_element_type=F32)


def wide_dot(left, right, left_dim, right_dim):
    return parts_dot(lay_left(split(left), left_dim), lay_right(split(right), right_dim), left_dim, right_dim)


def factor_block(rows, after):
    count = len(rows)
    rows = list(rows)
    lane = lax.broadcasted_iota(jnp.int32, (8, B), 1)
    sub = lax.broadcasted_iota(jnp.int32, (8, B), 0)

    def spread(v):
        return jnp.broadcast_to(v, (8, B))

    def columns(q, first):
        return [spread(rows[q][:, first + s : first + s + 1]) for s in range(8)]

    upper, inverse = [], []
    coming = columns(0, 0)
    for p in range(count):
        c0 = 8 * p
        inside = (lane >= c0) & (lane < c0 + 8)
        cols = coming
        own = jnp.where(inside, jnp.where(lane - c0 == sub, 1.0, 0.0), rows[p])
        last = p + 1 == count
        below = None if last else columns(p + 1, c0)
        coming = None if last else columns(p + 1, c0 + 8)
        pivots = jnp.zeros((8, B), F32)
        scales, ahead, pivot_rows = [], [], []
        for s in range(8):
            pivot = spread(cols[s][s : s + 1])
            pivots = jnp.where(sub == s, pivot, pivots)
            scales.append(1.0 / pivot)
            ahead.append([spread(cols[t][s : s + 1]) if t > s else None for t in range(8)])
            pivot_rows.append(spread(own[s : s + 1]))
            factor = jnp.where(sub > s, cols[s], 0.0) * scales[s]
            for t in range(s + 1, 8):
                cols[t] = cols[t] - factor * ahead[s][t]
            own = own - factor * pivot_rows[s]
        for q in range(p + 1, min(count, p + 1 + NEAR)):
            here = below if q == p + 1 else columns(q, c0)
            target = jnp.where(inside, 0.0, rows[q])
            for s in range(8):
                factor = here[s] * scales[s]
                for t in range(s + 1, 8):
                    here[t] = here[t] - factor * ahead[s][t]
                if q == p + 1:
                    coming = [coming[t] - factor * spread(here[s][t : t + 1]) for t in range(8)]
                target = target - factor * pivot_rows[s]
            rows[q] = target
        root = lax.rsqrt(pivots)
        root = root * (1.5 - 0.5 * pivots * root * root)
        scaled = own * root
        far = p + 1 + NEAR
        if far < count:
            update = wide_dot(scaled, scaled, 0, 0)
            for q in range(far, count):
                rows[q] = jnp.where(inside, 0.0, rows[q]) - update[8 * q : 8 * q + 8]
        u = own
        for t in range(8):
            u = jnp.where(lane == c0 + t, cols[t], u)
        upper.append(jnp.where(lane >= c0 + sub, u, 0.0) * root)
        inverse.append(jnp.where(lane <= c0 + sub, scaled, 0.0))
        after(p)
    return jnp.concatenate(upper, 0), jnp.concatenate(inverse, 0)


def gram_kernel(scale, core, x, mine, theirs, x_parts, parts):
    for h in range(STEPS // 2):
        for i, part in enumerate(split(jnp.concatenate([x[2 * h], x[2 * h + 1]], 1))):
            x_parts[i, :, 2 * h * B : 2 * h * B + 2 * B] = part.astype(BF16)
    wide = [[x_parts[i, :, 2 * h * B : 2 * h * B + 2 * B] for i in range(3)] for h in range(STEPS // 2)]
    turned = [lay_left([part.T for part in parts], 1) for parts in wide]
    for h, i in ((0, 0), (0, 1), (1, 1)):
        product = parts_dot(turned[h], lay_right(wide[i], 0)) * scale
        for k in (2 * h, 2 * h + 1):
            for j in (2 * i, 2 * i + 1):
                if j >= k:
                    parts[PAIRS.index((k, j))] = product[k % 2 * B : k % 2 * B + B, j % 2 * B : j % 2 * B + B]
    for owner, out in ((core[0], mine), (1 - core[0], theirs)):
        out[: BOTH * B, :] = parts[:BOTH].reshape(BOTH * B, B)
        out[BOTH * B :, :] = parts[pl.ds(BOTH + owner * HALF, HALF)].reshape(HALF * B, B)


def gram(core, x, scale):
    return pl.pallas_call(
        functools.partial(gram_kernel, scale),
        in_specs=[SMEM, VMEM],
        out_shape=[jax.ShapeDtypeStruct((OWN * B, B), F32)] * 2,
        scratch_shapes=[pltpu.VMEM((3, x.shape[1], N), BF16), pltpu.VMEM((len(PAIRS), B, B), F32)],
        compiler_params=pltpu.CompilerParams(vmem_limit_bytes=32 << 20),
        name="gram",
    )(core, x)


def first_kernel(mine, upper_ref, inverse_ref, panel_ref):
    upper, inverse = factor_block([mine[8 * q : 8 * q + 8, :] for q in range(B // 8)], lambda p: None)
    upper_ref[...] = upper
    inverse_ref[...] = inverse
    panel_ref[...] = wide_dot(inverse, mine[B : 2 * B, :], 1, 0)


def first(mine):
    return pl.pallas_call(
        first_kernel,
        in_specs=[VMEM],
        out_shape=[jax.ShapeDtypeStruct((B, B), F32)] * 3,
        compiler_params=pltpu.CompilerParams(vmem_limit_bytes=16 << 20),
        cost_estimate=pl.CostEstimate(flops=4 << 20, bytes_accessed=4 << 20, transcendentals=0),
        name="first",
    )(mine)


def factor_kernel(core, mine, theirs, upper0, inverse0, panel0, x, basis_ref, u_ref, m, rest, right, x_parts):
    todo = []

    def after(p):
        for _ in range(-(-len(todo) // (B // 8 - p))):
            todo.pop(0)()

    def block(k):
        return slice(k * B, k * B + B)

    def panel(k, j, inverse):
        r = wide_dot(inverse, m[block(k), block(j)], 1, 0)
        m[block(k), block(j)] = r
        if j > k:
            u_ref[block(k), block(j)] = r

    def trail(k, i, j):
        d = wide_dot(u_ref[block(k), block(i)], m[block(k), block(j)], 0, 0)
        m[block(i), block(j)] = -d if j == k else m[block(i), block(j)] - d

    def separate(g, rows):
        for i, part in enumerate(split(x[g, rows, :])):
            x_parts[i, rows, block(g)] = part.astype(BF16)

    def prepare(first_row, columns):
        v = m[first_row : first_row + 2 * B, :columns]
        right[:, : 6 * columns] = lay_right(split(v), 1)

    def product(rows, columns):
        left = lay_left([x_parts[i, rows, :columns] for i in range(3)], 1)
        return parts_dot(left, right[:, : 6 * columns], 1, 1)

    def basis_first(rows):
        basis_ref[rows, : 2 * B] = product(rows, 2 * B)

    def basis_last(rows):
        both = product(rows, 3 * B)
        basis_ref[rows, block(2)] = both[:, :B]
        rest[rows, :] = both[:, B:] + x[3, rows, :]

    chunks = [slice(c, c + 2 * B) for c in range(0, x.shape[1], 2 * B)]
    for k, j in PAIRS[BOTH:]:
        owner, at = divmod(PAIRS.index((k, j)) - BOTH, HALF)
        m[block(k), block(j)] = jnp.where(core[0] == owner, mine[block(BOTH + at), :], theirs[block(at), :])
    for k in range(STEPS):
        if k == 0:
            upper, inverse = upper0[...], inverse0[...]
        else:
            rows = [m[k * B + 8 * q : k * B + 8 * q + 8, block(k)] for q in range(B // 8)]
            upper, inverse = factor_block(rows, after)
        u_ref[block(k), block(k)] = upper
        for j in range(k):
            u_ref[block(k), block(j)] = jnp.zeros((B, B), F32)
        if k == 0:
            m[block(0), block(1)] = panel0[...]
            u_ref[block(0), block(1)] = panel0[...]
        elif k + 1 < STEPS:
            panel(k, k + 1, inverse)
        if k + 1 < STEPS:
            trail(k, k + 1, k + 1)
        m[block(k), block(k)] = inverse
        if k + 1 < STEPS:
            todo += [functools.partial(panel, k, j, inverse) for j in range(STEPS) if j not in (k, k + 1)]
        for i in range(k + 1, STEPS):
            for j in range(STEPS):
                if (j <= k or j >= i) and (i, j) != (k + 1, k + 1):
                    todo.append(functools.partial(trail, k, i, j))
        if k == 0:
            todo += [functools.partial(separate, g, rows) for g in range(STEPS - 1) for rows in chunks]
        if k == 1:
            m[block(0), block(1)] = jnp.zeros((B, B), F32)
            todo.append(functools.partial(prepare, 0, 2 * B))
            todo += [functools.partial(basis_first, rows) for rows in chunks]
        if k == 2:
            todo.append(functools.partial(prepare, 2 * B, 3 * B))
            todo += [functools.partial(basis_last, rows) for rows in chunks]
    basis_ref[:, block(3)] = wide_dot(rest[...], inverse, 1, 1)


def factor(core, mine, theirs, upper0, inverse0, panel0, x):
    return pl.pallas_call(
        factor_kernel,
        in_specs=[SMEM] + [VMEM] * 6,
        out_shape=[jax.ShapeDtypeStruct((x.shape[1], N), F32), jax.ShapeDtypeStruct((N, N), F32)],
        scratch_shapes=[
            pltpu.VMEM((N, N), F32),
            pltpu.VMEM((x.shape[1], B), F32),
            pltpu.VMEM((2 * B, 6 * 3 * B), BF16),
            pltpu.VMEM((3, x.shape[1], N), BF16),
        ],
        compiler_params=pltpu.CompilerParams(vmem_limit_bytes=32 << 20),
        name="factor",
    )(core, mine, theirs, upper0, inverse0, panel0, x)


def other_core(v):
    return lax.ppermute(v, "core", [(0, 1), (1, 0)])


def all_sum(mine, theirs):
    chips = ("x", "y", "z")
    mine = mine + other_core(theirs)
    peers = lax.axis_size(chips)
    pieces = mine.reshape(peers, OWN * B // peers, 1, B)
    pieces = lax.all_to_all(pieces, chips, split_axis=0, concat_axis=0, tiled=True)
    piece = jnp.sum(pieces, axis=0)
    pieces = jnp.broadcast_to(piece[None], (peers,) + piece.shape)
    pieces = lax.all_to_all(pieces, chips, split_axis=0, concat_axis=0, tiled=True)
    return pieces.reshape(OWN * B, B)


def local(sketch):
    groups = lax.axis_size("x")
    x = lax.all_to_all(sketch.reshape(groups, -1, B), "x", split_axis=0, concat_axis=0, tiled=True)
    total_rows = x.shape[1] * lax.axis_size(("x", "y", "z", "core"))
    core = lax.axis_index("core").reshape(1)
    mine, theirs = gram(core, x, 1.0 / total_rows)
    mine = all_sum(mine, theirs)
    theirs = other_core(mine[BOTH * B :])
    return factor(core, mine, theirs, *first(mine), x)


def solution(mesh):
    grp, row = mesh.devices.shape
    core = 2
    side = 8
    grid = Mesh(mesh.devices.reshape(grp, row // (side * core), side, core), ("x", "y", "z", "core"))
    row_axes = ("y", "z", "core")
    return jax.shard_map(
        local,
        mesh=grid,
        in_specs=(P(row_axes, "x"),),
        out_specs=(P(row_axes + ("x",), None), P()),
        check_vma=False,
    )
```

```python
import functools

import jax
import jax.numpy as jnp
from jax import lax
from jax.experimental import pallas as pl
from jax.experimental.pallas import tpu as pltpu
from jax.sharding import Mesh
from jax.sharding import PartitionSpec as P

B = 128
N = 512
STEPS = N // B
PAIRS = [(k, j) for k in range(STEPS) for j in range(k, STEPS)]
BOTH = 2
HALF = (len(PAIRS) - BOTH) // 2
OWN = BOTH + HALF
F32 = jnp.float32
BF16 = jnp.bfloat16
NEAR = 3
SMEM = pl.BlockSpec(memory_space=pltpu.SMEM)
VMEM = pl.BlockSpec(memory_space=pltpu.VMEM)


def split(v):
    high = v.astype(BF16).astype(F32)
    rest = v - high
    middle = rest.astype(BF16).astype(F32)
    return high, middle, rest - middle


def lay_left(parts, dim):
    a, b, c = parts
    return jnp.concatenate([a, a, b, b, a, c], dim).astype(BF16)


def lay_right(parts, dim):
    a, b, c = parts
    return jnp.concatenate([a, b, a, b, c, a], dim).astype(BF16)


def parts_dot(left, right, left_dim=1, right_dim=0):
    return lax.dot_general(left, right, (((left_dim,), (right_dim,)), ((), ())), preferred_element_type=F32)


def wide_dot(left, right, left_dim, right_dim):
    return parts_dot(lay_left(split(left), left_dim), lay_right(split(right), right_dim), left_dim, right_dim)


def factor_block(rows, after):
    count = len(rows)
    rows = list(rows)
    lane = lax.broadcasted_iota(jnp.int32, (8, B), 1)
    sub = lax.broadcasted_iota(jnp.int32, (8, B), 0)

    def spread(v):
        return jnp.broadcast_to(v, (8, B))

    def columns(q, first):
        return [spread(rows[q][:, first + s : first + s + 1]) for s in range(8)]

    upper, inverse = [], []
    coming = columns(0, 0)
    for p in range(count):
        c0 = 8 * p
        inside = (lane >= c0) & (lane < c0 + 8)
        cols = coming
        own = jnp.where(inside, jnp.where(lane - c0 == sub, 1.0, 0.0), rows[p])
        last = p + 1 == count
        below = None if last else columns(p + 1, c0)
        coming = None if last else columns(p + 1, c0 + 8)
        pivots = jnp.zeros((8, B), F32)
        scales, ahead, pivot_rows = [], [], []
        for s in range(8):
            pivot = spread(cols[s][s : s + 1])
            pivots = jnp.where(sub == s, pivot, pivots)
            scales.append(1.0 / pivot)
            ahead.append([spread(cols[t][s : s + 1]) if t > s else None for t in range(8)])
            pivot_rows.append(spread(own[s : s + 1]))
            factor = jnp.where(sub > s, cols[s], 0.0) * scales[s]
            for t in range(s + 1, 8):
                cols[t] = cols[t] - factor * ahead[s][t]
            own = own - factor * pivot_rows[s]
        for q in range(p + 1, min(count, p + 1 + NEAR)):
            here = below if q == p + 1 else columns(q, c0)
            target = jnp.where(inside, 0.0, rows[q])
            for s in range(8):
                factor = here[s] * scales[s]
                for t in range(s + 1, 8):
                    here[t] = here[t] - factor * ahead[s][t]
                if q == p + 1:
                    coming = [coming[t] - factor * spread(here[s][t : t + 1]) for t in range(8)]
                target = target - factor * pivot_rows[s]
            rows[q] = target
        root = lax.rsqrt(pivots)
        root = root * (1.5 - 0.5 * pivots * root * root)
        scaled = own * root
        far = p + 1 + NEAR
        if far < count:
            update = wide_dot(scaled, scaled, 0, 0)
            for q in range(far, count):
                rows[q] = jnp.where(inside, 0.0, rows[q]) - update[8 * q : 8 * q + 8]
        u = own
        for t in range(8):
            u = jnp.where(lane == c0 + t, cols[t], u)
        upper.append(jnp.where(lane >= c0 + sub, u, 0.0) * root)
        inverse.append(jnp.where(lane <= c0 + sub, scaled, 0.0))
        after(p)
    return jnp.concatenate(upper, 0), jnp.concatenate(inverse, 0)


def gram_kernel(scale, core, x, mine, theirs, x_parts, parts):
    for h in range(STEPS // 2):
        for i, part in enumerate(split(jnp.concatenate([x[2 * h], x[2 * h + 1]], 1))):
            x_parts[i, :, 2 * h * B : 2 * h * B + 2 * B] = part.astype(BF16)
    wide = [[x_parts[i, :, 2 * h * B : 2 * h * B + 2 * B] for i in range(3)] for h in range(STEPS // 2)]
    turned = [lay_left([part.T for part in parts], 1) for parts in wide]
    for h, i in ((0, 0), (0, 1), (1, 1)):
        product = parts_dot(turned[h], lay_right(wide[i], 0)) * scale
        for k in (2 * h, 2 * h + 1):
            for j in (2 * i, 2 * i + 1):
                if j >= k:
                    parts[PAIRS.index((k, j))] = product[k % 2 * B : k % 2 * B + B, j % 2 * B : j % 2 * B + B]
    for owner, out in ((core[0], mine), (1 - core[0], theirs)):
        out[: BOTH * B, :] = parts[:BOTH].reshape(BOTH * B, B)
        out[BOTH * B :, :] = parts[pl.ds(BOTH + owner * HALF, HALF)].reshape(HALF * B, B)


def gram(core, x, scale):
    return pl.pallas_call(
        functools.partial(gram_kernel, scale),
        in_specs=[SMEM, VMEM],
        out_shape=[jax.ShapeDtypeStruct((OWN * B, B), F32)] * 2,
        scratch_shapes=[pltpu.VMEM((3, x.shape[1], N), BF16), pltpu.VMEM((len(PAIRS), B, B), F32)],
        compiler_params=pltpu.CompilerParams(vmem_limit_bytes=32 << 20),
        name="gram",
    )(core, x)


def first_kernel(mine, upper_ref, inverse_ref, panel_ref):
    upper, inverse = factor_block([mine[8 * q : 8 * q + 8, :] for q in range(B // 8)], lambda p: None)
    upper_ref[...] = upper
    inverse_ref[...] = inverse
    panel_ref[...] = wide_dot(inverse, mine[B : 2 * B, :], 1, 0)


def first(mine):
    return pl.pallas_call(
        first_kernel,
        in_specs=[VMEM],
        out_shape=[jax.ShapeDtypeStruct((B, B), F32)] * 3,
        compiler_params=pltpu.CompilerParams(vmem_limit_bytes=16 << 20),
        cost_estimate=pl.CostEstimate(flops=4 << 20, bytes_accessed=4 << 20, transcendentals=0),
        name="first",
    )(mine)


def factor_kernel(core, mine, theirs, upper0, inverse0, panel0, x, basis_ref, u_ref, m, rest, right, x_parts):
    todo = []

    def after(p):
        for _ in range(-(-len(todo) // (B // 8 - p))):
            todo.pop(0)()

    def block(k):
        return slice(k * B, k * B + B)

    def panel(k, j, inverse):
        r = wide_dot(inverse, m[block(k), block(j)], 1, 0)
        m[block(k), block(j)] = r
        if j > k:
            u_ref[block(k), block(j)] = r

    def trail(k, i, j):
        d = wide_dot(u_ref[block(k), block(i)], m[block(k), block(j)], 0, 0)
        m[block(i), block(j)] = -d if j == k else m[block(i), block(j)] - d

    def separate(g, rows):
        for i, part in enumerate(split(x[g, rows, :])):
            x_parts[i, rows, block(g)] = part.astype(BF16)

    def prepare(first_row, columns):
        v = m[first_row : first_row + 2 * B, :columns]
        right[:, : 6 * columns] = lay_right(split(v), 1)

    def product(rows, columns):
        left = lay_left([x_parts[i, rows, :columns] for i in range(3)], 1)
        return parts_dot(left, right[:, : 6 * columns], 1, 1)

    def basis_first(rows):
        basis_ref[rows, : 2 * B] = product(rows, 2 * B)

    def basis_last(rows):
        both = product(rows, 3 * B)
        basis_ref[rows, block(2)] = both[:, :B]
        rest[rows, :] = both[:, B:] + x[3, rows, :]

    chunks = [slice(c, c + 2 * B) for c in range(0, x.shape[1], 2 * B)]
    for k, j in PAIRS[BOTH:]:
        owner, at = divmod(PAIRS.index((k, j)) - BOTH, HALF)
        m[block(k), block(j)] = jnp.where(core[0] == owner, mine[block(BOTH + at), :], theirs[block(at), :])
    for k in range(STEPS):
        if k == 0:
            upper, inverse = upper0[...], inverse0[...]
        else:
            rows = [m[k * B + 8 * q : k * B + 8 * q + 8, block(k)] for q in range(B // 8)]
            upper, inverse = factor_block(rows, after)
        u_ref[block(k), block(k)] = upper
        for j in range(k):
            u_ref[block(k), block(j)] = jnp.zeros((B, B), F32)
        if k == 0:
            m[block(0), block(1)] = panel0[...]
            u_ref[block(0), block(1)] = panel0[...]
        elif k + 1 < STEPS:
            panel(k, k + 1, inverse)
        if k + 1 < STEPS:
            trail(k, k + 1, k + 1)
        m[block(k), block(k)] = inverse
        if k + 1 < STEPS:
            todo += [functools.partial(panel, k, j, inverse) for j in range(STEPS) if j not in (k, k + 1)]
        for i in range(k + 1, STEPS):
            for j in range(STEPS):
                if (j <= k or j >= i) and (i, j) != (k + 1, k + 1):
                    todo.append(functools.partial(trail, k, i, j))
        if k == 0:
            todo += [functools.partial(separate, g, rows) for g in range(STEPS - 1) for rows in chunks]
        if k == 1:
            m[block(0), block(1)] = jnp.zeros((B, B), F32)
            todo.append(functools.partial(prepare, 0, 2 * B))
            todo += [functools.partial(basis_first, rows) for rows in chunks]
        if k == 2:
            todo.append(functools.partial(prepare, 2 * B, 3 * B))
            todo += [functools.partial(basis_last, rows) for rows in chunks]
    basis_ref[:, block(3)] = wide_dot(rest[...], inverse, 1, 1)


def factor(core, mine, theirs, upper0, inverse0, panel0, x):
    return pl.pallas_call(
        factor_kernel,
        in_specs=[SMEM] + [VMEM] * 6,
        out_shape=[jax.ShapeDtypeStruct((x.shape[1], N), F32), jax.ShapeDtypeStruct((N, N), F32)],
        scratch_shapes=[
            pltpu.VMEM((N, N), F32),
            pltpu.VMEM((x.shape[1], B), F32),
            pltpu.VMEM((2 * B, 6 * 3 * B), BF16),
            pltpu.VMEM((3, x.shape[1], N), BF16),
        ],
        compiler_params=pltpu.CompilerParams(vmem_limit_bytes=32 << 20),
        name="factor",
    )(core, mine, theirs, upper0, inverse0, panel0, x)


def other_core(v):
    return lax.ppermute(v, "core", [(0, 1), (1, 0)])


def all_sum(mine, theirs):
    chips = ("z", "y", "x")
    mine = mine + other_core(theirs)
    peers = lax.axis_size(chips)
    pieces = mine.reshape(peers, OWN * B // peers, 1, B)
    pieces = lax.all_to_all(pieces, chips, split_axis=0, concat_axis=0, tiled=True)
    piece = jnp.sum(pieces, axis=0)
    pieces = jnp.broadcast_to(piece[None], (peers,) + piece.shape)
    pieces = lax.all_to_all(pieces, chips, split_axis=0, concat_axis=0, tiled=True)
    return pieces.reshape(OWN * B, B)


def local(sketch):
    groups = lax.axis_size("x")
    x = lax.all_to_all(sketch.reshape(groups, -1, B), "x", split_axis=0, concat_axis=0, tiled=True)
    total_rows = x.shape[1] * lax.axis_size(("x", "y", "z", "core"))
    core = lax.axis_index("core").reshape(1)
    mine, theirs = gram(core, x, 1.0 / total_rows)
    mine = all_sum(mine, theirs)
    theirs = other_core(mine[BOTH * B :])
    return factor(core, mine, theirs, *first(mine), x)


def solution(mesh):
    grp, row = mesh.devices.shape
    core = 2
    side = 8
    grid = Mesh(mesh.devices.reshape(grp, row // (side * core), side, core), ("x", "y", "z", "core"))
    row_axes = ("y", "z", "core")
    return jax.shard_map(
        local,
        mesh=grid,
        in_specs=(P(row_axes, "x"),),
        out_specs=(P(row_axes + ("x",), None), P()),
        check_vma=False,
    )
```

```python
import functools

import jax
import jax.numpy as jnp
from jax import lax
from jax.experimental import pallas as pl
from jax.experimental.pallas import tpu as pltpu
from jax.sharding import Mesh
from jax.sharding import PartitionSpec as P

B = 128
N = 512
STEPS = N // B
PAIRS = [(k, j) for k in range(STEPS) for j in range(k, STEPS)]
BOTH = 2
HALF = (len(PAIRS) - BOTH) // 2
OWN = BOTH + HALF
F32 = jnp.float32
BF16 = jnp.bfloat16
NEAR = 3
SMEM = pl.BlockSpec(memory_space=pltpu.SMEM)
VMEM = pl.BlockSpec(memory_space=pltpu.VMEM)


def split(v):
    high = v.astype(BF16).astype(F32)
    rest = v - high
    middle = rest.astype(BF16).astype(F32)
    return high, middle, rest - middle


def lay_left(parts, dim):
    a, b, c = parts
    return jnp.concatenate([a, a, b, b, a, c], dim).astype(BF16)


def lay_right(parts, dim):
    a, b, c = parts
    return jnp.concatenate([a, b, a, b, c, a], dim).astype(BF16)


def parts_dot(left, right, left_dim=1, right_dim=0):
    return lax.dot_general(left, right, (((left_dim,), (right_dim,)), ((), ())), preferred_element_type=F32)


def wide_dot(left, right, left_dim, right_dim):
    return parts_dot(lay_left(split(left), left_dim), lay_right(split(right), right_dim), left_dim, right_dim)


def factor_block(rows, after):
    count = len(rows)
    rows = list(rows)
    lane = lax.broadcasted_iota(jnp.int32, (8, B), 1)
    sub = lax.broadcasted_iota(jnp.int32, (8, B), 0)

    def spread(v):
        return jnp.broadcast_to(v, (8, B))

    def columns(q, first):
        return [spread(rows[q][:, first + s : first + s + 1]) for s in range(8)]

    upper, inverse = [], []
    coming = columns(0, 0)
    for p in range(count):
        c0 = 8 * p
        inside = (lane >= c0) & (lane < c0 + 8)
        cols = coming
        own = jnp.where(inside, jnp.where(lane - c0 == sub, 1.0, 0.0), rows[p])
        last = p + 1 == count
        below = None if last else columns(p + 1, c0)
        coming = None if last else columns(p + 1, c0 + 8)
        pivots = jnp.zeros((8, B), F32)
        scales, ahead, pivot_rows = [], [], []
        for s in range(8):
            pivot = spread(cols[s][s : s + 1])
            pivots = jnp.where(sub == s, pivot, pivots)
            scales.append(1.0 / pivot)
            ahead.append([spread(cols[t][s : s + 1]) if t > s else None for t in range(8)])
            pivot_rows.append(spread(own[s : s + 1]))
            factor = jnp.where(sub > s, cols[s], 0.0) * scales[s]
            for t in range(s + 1, 8):
                cols[t] = cols[t] - factor * ahead[s][t]
            own = own - factor * pivot_rows[s]
        for q in range(p + 1, min(count, p + 1 + NEAR)):
            here = below if q == p + 1 else columns(q, c0)
            target = jnp.where(inside, 0.0, rows[q])
            for s in range(8):
                factor = here[s] * scales[s]
                for t in range(s + 1, 8):
                    here[t] = here[t] - factor * ahead[s][t]
                if q == p + 1:
                    coming = [coming[t] - factor * spread(here[s][t : t + 1]) for t in range(8)]
                target = target - factor * pivot_rows[s]
            rows[q] = target
        root = lax.rsqrt(pivots)
        root = root * (1.5 - 0.5 * pivots * root * root)
        scaled = own * root
        far = p + 1 + NEAR
        if far < count:
            update = wide_dot(scaled, scaled, 0, 0)
            for q in range(far, count):
                rows[q] = jnp.where(inside, 0.0, rows[q]) - update[8 * q : 8 * q + 8]
        u = own
        for t in range(8):
            u = jnp.where(lane == c0 + t, cols[t], u)
        upper.append(jnp.where(lane >= c0 + sub, u, 0.0) * root)
        inverse.append(jnp.where(lane <= c0 + sub, scaled, 0.0))
        after(p)
    return jnp.concatenate(upper, 0), jnp.concatenate(inverse, 0)


def gram_kernel(scale, owner, x, out):
    def fill(pairs, start):
        for k in range(STEPS):
            columns = [j for i, j in pairs if i == k]
            if columns:
                left = lay_left([part.astype(BF16).T for part in split(x[k])], 1)
                right = lay_right(split(jnp.concatenate([x[j] for j in columns], 1)), 0)
                product = parts_dot(left, right) * scale
                for n, j in enumerate(columns):
                    at = (start + pairs.index((k, j))) * B
                    out[at : at + B, :] = product[:, n * B : n * B + B]

    fill(PAIRS[:BOTH], 0)
    for which in range(2):
        own = BOTH + which * HALF
        pl.when(owner[0] == which)(functools.partial(fill, PAIRS[own : own + HALF], BOTH))


def gram(owner, x, scale):
    return pl.pallas_call(
        functools.partial(gram_kernel, scale),
        in_specs=[SMEM, VMEM],
        out_shape=jax.ShapeDtypeStruct((OWN * B, B), F32),
        compiler_params=pltpu.CompilerParams(vmem_limit_bytes=32 << 20),
        cost_estimate=pl.CostEstimate(flops=1 << 30, bytes_accessed=2 << 20, transcendentals=0),
        name="gram",
    )(owner, x)


def first_kernel(mine, upper_ref, inverse_ref, panel_ref):
    upper, inverse = factor_block([mine[8 * q : 8 * q + 8, :] for q in range(B // 8)], lambda p: None)
    upper_ref[...] = upper
    inverse_ref[...] = inverse
    panel_ref[...] = wide_dot(inverse, mine[B : 2 * B, :], 1, 0)


def first(mine):
    return pl.pallas_call(
        first_kernel,
        in_specs=[VMEM],
        out_shape=[jax.ShapeDtypeStruct((B, B), F32)] * 3,
        compiler_params=pltpu.CompilerParams(vmem_limit_bytes=16 << 20),
        cost_estimate=pl.CostEstimate(flops=4 << 20, bytes_accessed=4 << 20, transcendentals=0),
        name="first",
    )(mine)


def factor_kernel(core, mine, theirs, upper0, inverse0, panel0, x, basis_ref, u_ref, m, rest, right, x_parts):
    todo = []

    def after(p):
        for _ in range(-(-len(todo) // (B // 8 - p))):
            todo.pop(0)()

    def block(k):
        return slice(k * B, k * B + B)

    def panel(k, j, inverse):
        r = wide_dot(inverse, m[block(k), block(j)], 1, 0)
        m[block(k), block(j)] = r
        if j > k:
            u_ref[block(k), block(j)] = r

    def trail(k, i, j):
        d = wide_dot(u_ref[block(k), block(i)], m[block(k), block(j)], 0, 0)
        m[block(i), block(j)] = -d if j == k else m[block(i), block(j)] - d

    def separate(g, rows):
        for i, part in enumerate(split(x[g, rows, :])):
            x_parts[i, rows, block(g)] = part.astype(BF16)

    def prepare(first_row, columns):
        v = m[first_row : first_row + 2 * B, :columns]
        right[:, : 6 * columns] = lay_right(split(v), 1)

    def product(rows, columns):
        left = lay_left([x_parts[i, rows, :columns] for i in range(3)], 1)
        return parts_dot(left, right[:, : 6 * columns], 1, 1)

    def basis_first(rows):
        basis_ref[rows, : 2 * B] = product(rows, 2 * B)

    def basis_last(rows):
        both = product(rows, 3 * B)
        basis_ref[rows, block(2)] = both[:, :B]
        rest[rows, :] = both[:, B:] + x[3, rows, :]

    chunks = [slice(c, c + 2 * B) for c in range(0, x.shape[1], 2 * B)]
    for k, j in PAIRS[BOTH:]:
        owner, at = divmod(PAIRS.index((k, j)) - BOTH, HALF)
        m[block(k), block(j)] = jnp.where(core[0] == owner, mine[block(BOTH + at), :], theirs[block(at), :])
    for k in range(STEPS):
        if k == 0:
            upper, inverse = upper0[...], inverse0[...]
        else:
            rows = [m[k * B + 8 * q : k * B + 8 * q + 8, block(k)] for q in range(B // 8)]
            upper, inverse = factor_block(rows, after)
        u_ref[block(k), block(k)] = upper
        for j in range(k):
            u_ref[block(k), block(j)] = jnp.zeros((B, B), F32)
        if k == 0:
            m[block(0), block(1)] = panel0[...]
            u_ref[block(0), block(1)] = panel0[...]
        elif k + 1 < STEPS:
            panel(k, k + 1, inverse)
        if k + 1 < STEPS:
            trail(k, k + 1, k + 1)
        m[block(k), block(k)] = inverse
        if k + 1 < STEPS:
            todo += [functools.partial(panel, k, j, inverse) for j in range(STEPS) if j not in (k, k + 1)]
        for i in range(k + 1, STEPS):
            for j in range(STEPS):
                if (j <= k or j >= i) and (i, j) != (k + 1, k + 1):
                    todo.append(functools.partial(trail, k, i, j))
        if k == 0:
            todo += [functools.partial(separate, g, rows) for g in range(STEPS - 1) for rows in chunks]
        if k == 1:
            m[block(0), block(1)] = jnp.zeros((B, B), F32)
            todo.append(functools.partial(prepare, 0, 2 * B))
            todo += [functools.partial(basis_first, rows) for rows in chunks]
        if k == 2:
            todo.append(functools.partial(prepare, 2 * B, 3 * B))
            todo += [functools.partial(basis_last, rows) for rows in chunks]
    basis_ref[:, block(3)] = wide_dot(rest[...], inverse, 1, 1)


def factor(core, mine, theirs, upper0, inverse0, panel0, x):
    return pl.pallas_call(
        factor_kernel,
        in_specs=[SMEM] + [VMEM] * 6,
        out_shape=[jax.ShapeDtypeStruct((x.shape[1], N), F32), jax.ShapeDtypeStruct((N, N), F32)],
        scratch_shapes=[
            pltpu.VMEM((N, N), F32),
            pltpu.VMEM((x.shape[1], B), F32),
            pltpu.VMEM((2 * B, 6 * 3 * B), BF16),
            pltpu.VMEM((3, x.shape[1], N), BF16),
        ],
        compiler_params=pltpu.CompilerParams(vmem_limit_bytes=32 << 20),
        name="factor",
    )(core, mine, theirs, upper0, inverse0, panel0, x)


def other_core(v):
    return lax.ppermute(v, "core", [(0, 1), (1, 0)])


def all_sum(mine):
    chips = ("z", "y", "x")
    peers = lax.axis_size(chips)
    pieces = mine.reshape(peers, OWN * B // peers, 1, B)
    pieces = lax.all_to_all(pieces, chips, split_axis=0, concat_axis=0, tiled=True)
    piece = jnp.sum(pieces, axis=0)
    pieces = jnp.broadcast_to(piece[None], (peers,) + piece.shape)
    pieces = lax.all_to_all(pieces, chips, split_axis=0, concat_axis=0, tiled=True)
    return pieces.reshape(OWN * B, B)


def local(sketch):
    groups = lax.axis_size("x")
    x = lax.all_to_all(sketch.reshape(groups, -1, B), "x", split_axis=0, concat_axis=0, tiled=True)
    total_rows = x.shape[1] * lax.axis_size(("x", "y", "z", "core"))
    core = lax.axis_index("core").reshape(1)
    received = other_core(gram(1 - core, x, 1.0 / total_rows))
    mine = all_sum(gram(core, x, 1.0 / total_rows) + received)
    theirs = other_core(mine[BOTH * B :])
    return factor(core, mine, theirs, *first(mine), x)


def solution(mesh):
    grp, row = mesh.devices.shape
    core = 2
    side = 8
    grid = Mesh(mesh.devices.reshape(grp, row // (side * core), side, core), ("x", "y", "z", "core"))
    row_axes = ("y", "z", "core")
    return jax.shard_map(
        local,
        mesh=grid,
        in_specs=(P(row_axes, "x"),),
        out_specs=(P(row_axes + ("x",), None), P()),
        check_vma=False,
    )
```
